32 devices in a mesh: pair: 16 (over z, y, x), virt: 2 (over core).
Axes of the slice: x: 2, y: 2, z: 4, core: 2. Of those that a mesh axis runs over, the one named last changes fastest.
Arguments:
- amplitudes: bfloat16 [128, 2, 4096], P('pair', 'virt'), may hold values from -6 to 6
- partner: int32 [128], P('pair'), may hold values from 0 to 127, as said below
- integrals: bfloat16 [16, 4096, 4096], P('virt', 'pair'), may hold values from -0.09375 to 0.09375
- pattern: int32 [16], P('virt'), may hold values from 0 to 3, as said below
- owner: int32 [4], replicated, may hold values from 0 to 3, as said below
Outputs:
- ladder: bfloat16 [128, 4, 4096], P('pair', 'virt')
The draws below stay inside these ranges and needn't reach their ends.
Inputs may be any that keep to these rules, and one draw needn't show every extreme that they name: partner pairs each pair with another one and is its own inverse; the partner of a pair held by index j of pair is held by index j + 16 / 2 modulo 16, that is half the pair axis away. `pattern`: every ab tile pair appears exactly four times in all. owner names every ab tile pair exactly once.
All inputs are finite; a program needn't handle non-finite values.
Results may differ from the reference program's by a relative error of at most 0.0051.
Values may be sent and summed in bfloat16 or wider, within the bound.
No kernel may reach another device: no remote copies, remote signals or barrier semaphores. Data moves between devices by JAX's collectives and lax.ppermute only.
A program may use at most 64 MiB of HBM per device.

```python
import jax
import jax.numpy as jnp
from jax import lax

TILE = 64
TT = 4096
PAIR_DEV = 8
NNZ_DEV = 8
PAIRS = 128
NAB = 4
N_PAIR = 16
N_VIRT = 2


def draw_partner(key, part):
    half = N_PAIR // 2
    keys = jax.random.split(jax.random.fold_in(key, 11), half)
    perms = jax.vmap(lambda one: jax.random.permutation(one, PAIR_DEV))(keys).astype(jnp.int32)
    inverse = jnp.argsort(perms, axis=1, stable=True).astype(jnp.int32)
    blocks = jnp.arange(half, dtype=jnp.int32)[:, None]
    lower = (blocks + half) * PAIR_DEV + perms
    upper = blocks * PAIR_DEV + inverse
    return jnp.concatenate([lower.reshape(-1), upper.reshape(-1)]).astype(jnp.int32)


def draw_pattern(key, part):
    total = N_VIRT * NNZ_DEV
    slots = jnp.arange(total, dtype=jnp.int32) % NAB
    shuffle = jax.random.permutation(jax.random.fold_in(key, 23), total).astype(jnp.int32)
    return jnp.take(slots, shuffle).astype(jnp.int32)


def draw_owner(key, part):
    return jax.random.permutation(jax.random.fold_in(key, 37), NAB).astype(jnp.int32)


def block_levels(own_key, dims, pieces, smallest, high):
    gain = 1.0
    for dim, blocks in pieces:
        draws = jax.random.uniform(jax.random.fold_in(jax.random.fold_in(own_key, 6), dim), (blocks,), jnp.float32, smallest / len(pieces), high / len(pieces))
        gain = gain * jnp.repeat(jnp.exp(draws), dims[dim] // blocks).reshape((-1,) + (1,) * (len(dims) - 1 - dim))
    return gain


def bell_draw(key, shape, deviation, reach, pieces=(), kind=jnp.bfloat16):
    factor_of = block_levels(key, shape, pieces, -0.22, 0.18) if pieces else 1.0
    drawn = jax.random.normal(key, shape, jnp.float32) * deviation * factor_of
    return jnp.minimum(jnp.maximum(drawn, -reach), reach).astype(kind)


def setup_inputs(seed: int = 0) -> dict:
    streams_of = jax.random.split(jax.random.key(seed), 6)
    amplitudes = bell_draw(streams_of[0], (PAIRS, N_VIRT, TT), 1.0, 6.0, ((0, 16), (1, 2)))
    partner = draw_partner(jax.random.fold_in(streams_of[5], 71), 0)
    integrals = bell_draw(streams_of[2], (N_VIRT * NNZ_DEV, TT, TT), TT ** -0.5, 0.09375, ((0, 2), (1, 16)))
    pattern = draw_pattern(jax.random.fold_in(streams_of[5], 71), 0)
    owner = draw_owner(jax.random.fold_in(streams_of[5], 71), 0)
    return dict(amplitudes=amplitudes, partner=partner, integrals=integrals, pattern=pattern, owner=owner)


def reference(amplitudes, partner, integrals, pattern, owner):
    mirror = jnp.take(amplitudes, partner, axis=0).reshape(PAIRS, N_VIRT, TILE, TILE)
    mirror = jnp.swapaxes(mirror, 2, 3).reshape(PAIRS, N_VIRT, TT)
    symmetric = (amplitudes.astype(jnp.float32) + mirror.astype(jnp.float32)).astype(jnp.bfloat16)

    def add_tile(total, index):
        column = (index // NNZ_DEV).astype(jnp.int32)
        left = lax.dynamic_index_in_dim(symmetric, column, axis=1, keepdims=False)
        right = lax.dynamic_index_in_dim(integrals, index, axis=0, keepdims=False)
        term = jnp.dot(left, right.T, preferred_element_type=jnp.float32)
        target = pattern[index].astype(jnp.int32)
        current = lax.dynamic_index_in_dim(total, target, axis=1, keepdims=False)
        total = lax.dynamic_update_index_in_dim(total, current + term, target, 1)
        return total, None

    summed = jnp.zeros((PAIRS, NAB, TT), jnp.float32)
    summed, unused = lax.scan(add_tile, summed, jnp.arange(N_VIRT * NNZ_DEV, dtype=jnp.int32))
    return jnp.take(summed, owner, axis=1).astype(jnp.bfloat16)
```

```python
import functools

import jax
import jax.numpy as jnp
from jax import lax
from jax.experimental import pallas as pl
from jax.experimental.pallas import tpu as pltpu
from jax.sharding import PartitionSpec as P

TILE = 64
LANES = 128
CHUNK = 4
SMALL = 2 * 2**20
MEDIUM = 8 * 2**20
LARGE = 28 * 2**20


def exchange(value, axis, mask):
    pairs = [(source, source ^ mask) for source in range(lax.axis_size(axis))]
    return lax.ppermute(value, axis, pairs)


def gather_half(piece, half):
    bits = [1 << n for n in range(half.bit_length() - 1)]
    pieces = {0: piece}
    for mask in sorted(range(1, half), key=lambda mask: bin(mask).count("1") == 2):
        spans = [bit for bit in bits if mask & bit]
        if len(spans) == 2:
            last = spans[0] if spans[1] == 2 * spans[0] else spans[1]
            pieces[mask] = exchange(pieces[mask ^ last], "pair", last)
        else:
            pieces[mask] = exchange(piece, "pair", mask)
    return [pieces[mask] for mask in range(half)]


def listed(index, size):
    inner = 1 << (size.bit_length() - 1) // 2
    away = index // inner - size // inner // 2
    rank = 2 * abs(away) - (away < 0)
    return rank * inner + inner - 1 - index % inner


def rotate(value, axis, step):
    size = lax.axis_size(axis)
    pairs = [(source, (source + step) % size) for source in range(size)]
    return lax.ppermute(value, axis, pairs)


def first_tiles(tiles):
    return jnp.where(early(), tiles, tiles * 5 // 8)


def find_places(pattern, owner, places, filled, share):
    tiles, slots = places.shape[0], filled.shape[0]
    shift = slots - lax.axis_index("virt") * share
    for s in range(slots):
        filled[s] = 0
    for k in range(tiles):
        place = jnp.int32(0)
        for s in range(slots):
            place = jnp.where(owner[s] == pattern[k], s, place)
        places[k] = lax.rem(place + shift, slots)


def stream(k, integrals, stage, arrived):
    return pltpu.make_async_copy(integrals.at[k], stage.at[k], arrived.at[k])


def add_tiles(first, last, integrals, stage, arrived, summed, places, filled):
    step = 32

    def tile(k, carry):
        stream(k, integrals, stage, arrived).wait()
        slot = places[k]
        seen = filled[slot]
        filled[slot] = 1

        def put(i, carry):
            here = pl.ds(pl.multiple_of(i * step, step), step)
            summed[slot, here] = stage[k, here]
            return carry

        def add(i, carry):
            here = pl.ds(pl.multiple_of(i * step, step), step)
            summed[slot, here] += stage[k, here]
            return carry

        @pl.when(seen == 0)
        def store():
            lax.fori_loop(0, summed.shape[1] // step, put, 0)

        @pl.when(seen == 1)
        def later():
            lax.fori_loop(0, summed.shape[1] // step, add, 0)

        return carry

    lax.fori_loop(first, last, tile, 0)


def start_tiles(first, last, integrals, stage, arrived):
    def start(k, carry):
        stream(k, integrals, stage, arrived).start()
        return carry

    lax.fori_loop(first, last, start, 0)


def prepare_kernel(
    share,
    partner_hbm,
    pattern_hbm,
    owner_hbm,
    plain_hbm,
    integrals,
    flipped,
    summed,
    source,
    pick,
    partner,
    pattern,
    owner,
    places,
    filled,
    plain,
    stage,
    by_c,
    by_pair,
    arrived,
    ready,
):
    rows, width = plain.shape
    pairs = width // LANES
    tiles, columns = integrals.shape[:2]
    slots = owner_hbm.shape[0]
    inputs = ((plain_hbm, plain), (pattern_hbm, pattern), (owner_hbm, owner), (partner_hbm, partner))
    copies = [pltpu.make_async_copy(old, new, ready.at[n]) for n, (old, new) in enumerate(inputs)]
    for copy in copies:
        copy.start()
    first = first_tiles(tiles)
    start_tiles(0, first, integrals, stage, arrived)
    copies[0].wait()
    lane = lax.broadcasted_iota(jnp.int32, (rows, LANES), 1)
    for g in range(pairs):
        block = plain[:, g * LANES : (g + 1) * LANES].astype(jnp.float32)
        by_c[(2 * g) * rows : (2 * g + 1) * rows, :] = block
        by_c[(2 * g + 1) * rows : (2 * g + 2) * rows, :] = pltpu.roll(block, TILE, 1)
    for p in range(rows):
        matrix = by_c[pl.ds(p, TILE, stride=rows), :]
        by_pair[p * TILE : (p + 1) * TILE, 0:TILE] = matrix[:, 0:TILE].T
    for g in range(pairs):
        even = by_pair[pl.ds(2 * g, rows, stride=TILE), :]
        odd = by_pair[pl.ds(2 * g + 1, rows, stride=TILE), :]
        flipped[:, g * LANES : (g + 1) * LANES] = jnp.where(lane < TILE, even, pltpu.roll(odd, TILE, 1))
    for copy in copies[1:]:
        copy.wait()
    row = lax.broadcasted_iota(jnp.int32, source.shape, 0)
    chosen = row
    for p in range(rows):
        chosen = jnp.where(row == p, lax.rem(partner[p], rows), chosen)
    source[...] = chosen
    depth = rows * share
    row = lax.broadcasted_iota(jnp.int32, (depth, depth), 0)
    col = lax.broadcasted_iota(jnp.int32, (depth, depth), 1)
    pair, slot = row // share, lax.rem(row, share)
    target = pair
    for p in range(rows):
        target = jnp.where(pair == p, lax.rem(partner[p], rows), target)
    pick[0] = (col == slot * rows + pair).astype(pick.dtype)
    pick[1] = (col == slot * rows + target).astype(pick.dtype)
    find_places(pattern, owner, places, filled, share)
    for s in range(slots):
        present = functools.reduce(jnp.logical_or, [places[k] == s for k in range(tiles)])

        @pl.when(jnp.logical_not(present))
        def empty():
            summed[s] = jnp.zeros(summed.shape[1:], summed.dtype)

    add_tiles(0, first, integrals, stage, arrived, summed, places, filled)


def prepare(partner, pattern, owner, plain, integrals, share):
    rows, width = plain.shape
    tiles, columns = integrals.shape[:2]
    slots = owner.shape[0]
    depth = rows * share
    vmem = pl.BlockSpec(memory_space=pltpu.VMEM)
    inputs = (partner, pattern, owner, plain, integrals)
    return pl.pallas_call(
        functools.partial(prepare_kernel, share),
        out_shape=(
            jax.ShapeDtypeStruct(plain.shape, jnp.float32),
            pltpu.VMEM((slots, columns, width), integrals.dtype),
            jax.ShapeDtypeStruct((rows, LANES), jnp.int32),
            jax.ShapeDtypeStruct((2, depth, depth), jnp.bfloat16),
        ),
        in_specs=[pl.BlockSpec(memory_space=pl.ANY)] * len(inputs),
        out_specs=(vmem, vmem, vmem, vmem),
        scratch_shapes=[
            pltpu.SMEM(partner.shape, jnp.int32),
            pltpu.SMEM(pattern.shape, jnp.int32),
            pltpu.SMEM(owner.shape, jnp.int32),
            pltpu.SMEM(pattern.shape, jnp.int32),
            pltpu.SMEM(owner.shape, jnp.int32),
            pltpu.VMEM(plain.shape, plain.dtype),
            pltpu.VMEM(integrals.shape, integrals.dtype),
            pltpu.VMEM((TILE * rows, LANES), jnp.float32),
            pltpu.VMEM((TILE * rows, LANES), jnp.float32),
            pltpu.SemaphoreType.DMA((tiles,)),
            pltpu.SemaphoreType.DMA((len(inputs) - 1,)),
        ],
        compiler_params=pltpu.CompilerParams(vmem_limit_bytes=LARGE),
        cost_estimate=pl.CostEstimate(flops=integrals.size, bytes_accessed=integrals.size, transcendentals=0),
        name="prepare",
    )(*[in_hbm(value) for value in inputs])


def complete_kernel(
    share, pattern_hbm, owner_hbm, integrals, started, after, summed, pattern, owner, places, filled, stage, arrived, ready
):
    tiles = integrals.shape[0]
    first = first_tiles(tiles)
    copies = [
        pltpu.make_async_copy(pattern_hbm, pattern, ready.at[0]),
        pltpu.make_async_copy(owner_hbm, owner, ready.at[1]),
    ]

    def fill(k, carry):
        filled[places[k]] = 1
        return carry

    @pl.when(first < tiles)
    def other_tiles():
        for copy in copies:
            copy.start()
        start_tiles(first, tiles, integrals, stage, arrived)
        for copy in copies:
            copy.wait()
        find_places(pattern, owner, places, filled, share)
        lax.fori_loop(0, first, fill, 0)
        add_tiles(first, tiles, integrals, stage, arrived, summed, places, filled)


def complete(pattern, owner, integrals, started, after, share):
    tiles, columns, width = integrals.shape
    vmem = pl.BlockSpec(memory_space=pltpu.VMEM)
    anywhere = pl.BlockSpec(memory_space=pl.ANY)
    return pl.pallas_call(
        functools.partial(complete_kernel, share),
        out_shape=pltpu.VMEM(started.shape, started.dtype),
        in_specs=[anywhere, anywhere, anywhere, vmem, anywhere],
        out_specs=vmem,
        scratch_shapes=[
            pltpu.SMEM(pattern.shape, jnp.int32),
            pltpu.SMEM(owner.shape, jnp.int32),
            pltpu.SMEM(pattern.shape, jnp.int32),
            pltpu.SMEM(owner.shape, jnp.int32),
            pltpu.VMEM(integrals.shape, integrals.dtype),
            pltpu.SemaphoreType.DMA((tiles,)),
            pltpu.SemaphoreType.DMA((2,)),
        ],
        input_output_aliases={3: 0},
        compiler_params=pltpu.CompilerParams(vmem_limit_bytes=LARGE),
        cost_estimate=pl.CostEstimate(flops=integrals.size, bytes_accessed=integrals.size, transcendentals=0),
        name="complete",
    )(in_hbm(pattern), in_hbm(owner), in_hbm(integrals), pltpu.with_memory_space_constraint(started, pltpu.VMEM), after)


def in_hbm(value):
    return pltpu.with_memory_space_constraint(value, pltpu.HBM)


def join_kernel(source, flipped, other, out):
    for g in range(other.shape[1] // LANES):
        here = slice(g * LANES, (g + 1) * LANES)
        picked = jnp.take_along_axis(other[:, here].astype(jnp.float32), source[...], axis=0)
        out[:, here] = (flipped[:, here] + picked).astype(out.dtype)


def join(source, flipped, other):
    vmem = pl.BlockSpec(memory_space=pltpu.VMEM)
    return pl.pallas_call(
        join_kernel,
        out_shape=jax.ShapeDtypeStruct(other.shape, other.dtype),
        in_specs=[vmem, vmem, vmem],
        out_specs=vmem,
        compiler_params=pltpu.CompilerParams(vmem_limit_bytes=SMALL),
        cost_estimate=pl.CostEstimate(flops=other.size * 2, bytes_accessed=other.size * 8, transcendentals=0),
        name="join",
    )(source, flipped, other)


def contract_kernel(half, virts, summed, *rest):
    pieces, (weights, theirs, turned) = rest[:half], rest[half:]
    slots, columns, width = summed.shape
    rows = pieces[0].shape[0]
    share = slots // virts
    count = half * rows
    groups = 2 * count // LANES

    def turn(g, carry):
        here = pl.ds(pl.multiple_of(g * LANES, LANES), LANES)
        block = jnp.concatenate([piece[:, here].astype(jnp.float32) for piece in pieces], axis=0).astype(jnp.bfloat16)
        doubled = jnp.concatenate([block, block], axis=0)
        for part in range(groups):
            turned[part, here, :] = doubled[part * LANES : (part + 1) * LANES].T.astype(jnp.float32)
        return carry

    lax.fori_loop(0, width // LANES, turn, 0, unroll=True)
    lane = lax.broadcasted_iota(jnp.int32, (TILE, LANES), 1)
    term = [jnp.zeros((share * columns, 2 * count), jnp.float32) for r in range(1, virts)]
    for first in range(0, width // TILE, CHUNK):
        here = slice(first * TILE, (first + CHUNK) * TILE)
        parts = []
        for part in range(groups):
            values = []
            for c in range(first, first + CHUNK):
                straight = turned[part, c * TILE : (c + 1) * TILE, :]
                back = turned.at[part][pl.ds(c, TILE, stride=TILE), :]
                values.append(jnp.where(lane + part * LANES < count, straight, back))
            parts.append(jnp.concatenate(values, axis=0).astype(weights.dtype))
        chunk = jnp.concatenate(parts, axis=1)
        weights[here, :] = chunk
        for r in range(1, virts):
            tiles = summed[r * share : (r + 1) * share, :, here].reshape(share * columns, CHUNK * TILE)
            term[r - 1] += jnp.dot(tiles, chunk, preferred_element_type=jnp.float32)
    for r in range(1, virts):
        send_home(term[r - 1], theirs.at[r - 1], half, rows, columns)


def early():
    return lax.rem(lax.axis_index("virt"), 2) == 1


def send_home(term, blocks, half, rows, columns):
    place = lax.axis_index("pair")
    inside, upper = lax.rem(place, half), place // half
    share = term.shape[0] // columns
    parts = [term[s * columns : (s + 1) * columns].T.reshape(2 * half, rows, columns) for s in range(share)]
    block = jnp.concatenate(parts, axis=1)
    for m in range(half):
        inner = inside ^ m
        for n, home in ((m, inner + (1 - upper) * half), (half + m, inner + upper * half)):
            blocks[listed(home, 2 * half)] = block[n].astype(blocks.dtype)


def own_kernel(half, rows, share, summed, weights, mine):
    columns, width = summed.shape[1:]
    tiles = summed[0:share].reshape(share * columns, width)
    send_home(jnp.dot(tiles, weights[...], preferred_element_type=jnp.float32), mine, half, rows, columns)


def own(summed, weights, half, rows, share):
    slots, columns, width = summed.shape
    vmem = pl.BlockSpec(memory_space=pltpu.VMEM)
    return pl.pallas_call(
        functools.partial(own_kernel, half, rows, share),
        out_shape=jax.ShapeDtypeStruct((2 * half, share * rows, columns), jnp.float32),
        in_specs=[vmem, vmem],
        out_specs=vmem,
        compiler_params=pltpu.CompilerParams(vmem_limit_bytes=MEDIUM),
        cost_estimate=pl.CostEstimate(
            flops=2 * share * columns * width * weights.shape[1], bytes_accessed=2 * weights.size, transcendentals=0
        ),
        name="own",
    )(pltpu.with_memory_space_constraint(summed, pltpu.VMEM), pltpu.with_memory_space_constraint(weights, pltpu.VMEM))


def contract(summed, pieces, virts):
    slots, columns, width = summed.shape
    half, rows = len(pieces), pieces[0].shape[0]
    count = 2 * half * rows
    share = slots // virts
    vmem = pl.BlockSpec(memory_space=pltpu.VMEM)
    return pl.pallas_call(
        functools.partial(contract_kernel, half, virts),
        out_shape=(
            pltpu.VMEM((width, count), jnp.bfloat16),
            jax.ShapeDtypeStruct((virts - 1, 2 * half, share * rows, columns), jnp.bfloat16),
        ),
        in_specs=[vmem] * (1 + len(pieces)),
        out_specs=(vmem, vmem),
        scratch_shapes=[
            pltpu.VMEM((count // LANES, width, LANES), jnp.float32),
        ],
        compiler_params=pltpu.CompilerParams(vmem_limit_bytes=LARGE),
        cost_estimate=pl.CostEstimate(
            flops=2 * summed.size * count, bytes_accessed=2 * summed.size, transcendentals=0
        ),
        name="contract",
    )(pltpu.with_memory_space_constraint(summed, pltpu.VMEM), *pieces)


def arrange_kernel(pick, received, out):
    sources, depth, columns = received.shape
    rows, share, width = out.shape
    half = sources // 2
    upper = lax.axis_index("pair") // half
    for source in range(sources):
        chosen = pick[jnp.where(upper == source // half, 0, 1)]
        value = jnp.dot(chosen, received[listed(source, sources)], preferred_element_type=jnp.float32)
        here = slice(source * columns, (source + 1) * columns)
        for r in range(rows):
            out[r, :, here] = value[r * share : (r + 1) * share].astype(out.dtype)


def arrange(pick, received, rows, share):
    sources, depth, columns = received.shape
    vmem = pl.BlockSpec(memory_space=pltpu.VMEM)
    return pl.pallas_call(
        arrange_kernel,
        out_shape=jax.ShapeDtypeStruct((rows, share, sources * columns), received.dtype),
        in_specs=[vmem, vmem],
        out_specs=vmem,
        compiler_params=pltpu.CompilerParams(vmem_limit_bytes=SMALL),
        cost_estimate=pl.CostEstimate(flops=2 * received.size, bytes_accessed=4 * received.size, transcendentals=0),
        name="arrange",
    )(pick, received)


def shards(amplitudes, partner, integrals, pattern, owner):
    half = lax.axis_size("pair") // 2
    virts = lax.axis_size("virt")
    rows = amplitudes.shape[0]
    share = owner.shape[0] // virts
    plain = amplitudes.reshape(rows, -1)
    other = exchange(plain, "pair", half)
    flipped, started, source, pick = prepare(partner, pattern, owner, plain, integrals, share)
    pieces = gather_half(join(source, flipped, other), half)
    summed = complete(pattern, owner, integrals, started, pieces[1], share)
    weights, theirs = contract(summed, pieces, virts)
    others = [rotate(theirs[r - 1], "virt", r) for r in range(1, virts)]
    mine = own(summed, weights, half, rows, share)
    for other in others:
        mine = mine + other.astype(jnp.float32)
    order = sorted(range(2 * half), key=lambda index: listed(index, 2 * half))
    received = lax.all_to_all(
        mine.astype(jnp.bfloat16), "pair", split_axis=0, concat_axis=0, tiled=True, axis_index_groups=[order]
    )
    return arrange(pick, received, rows, share)


def solution(mesh):
    return jax.shard_map(
        shards,
        mesh=mesh,
        in_specs=(P("pair", "virt", None), P("pair"), P("virt", "pair", None), P("virt"), P()),
        out_specs=P("pair", "virt", None),
        check_vma=False,
    )
```
